256 devices in a mesh: win: 32 (over z, x_lo, core), head: 8 (over y, x_hi).
Axes of the slice: x: 4 (x_hi: 2, x_lo: 2; x = x_hi * 2 + x_lo), y: 4, z: 8, core: 2. Of those that a mesh axis runs over, the one named last changes fastest.
Arguments:
- query_tokens: bfloat16 [32, 1152, 5120], P('win', None, 'head'), may hold values from -20 to 20
- key_tokens: bfloat16 [32, 1152, 5120], P('win', None, 'head'), may hold values from -20 to 20
- value_tokens: bfloat16 [32, 1152, 5120], P('win', None, 'head'), may hold values from -6 to 6
- context_index: int32 [32, 16], replicated, may hold values from -1 to 383, as said below
- window_start: int32 [32], replicated, may hold values from 0 to 255, as said below
Outputs:
- blended_out: bfloat16 [32, 1152, 5120], P('win', None, 'head')
The draws below stay inside these ranges and needn't reach their ends.
Inputs may be any that keep to these rules, and one draw needn't show every extreme that they name: `context_index`: -1 marks an unused slot. The used slots of a window name distinct windows other than itself, always include a frame of each of the next two windows (counted round the end), and number 2 to 16, 16 in some window and 2 in another. The frames named of any one window are exactly 2 distinct ones; the last frame of the last window is named. `window_start`: window w starts at a position from w * 8 to w * 8 + 7; the first window starts at 0 and the last at the end of its range.
All inputs are finite; a program needn't handle non-finite values.
Results may differ from the reference program's by a relative error of at most 0.0046.
Values may be sent and summed in bfloat16 or wider, within the bound.
No kernel may reach another device: no remote copies, remote signals or barrier semaphores. Data moves between devices by JAX's collectives and lax.ppermute only.
A program may use at most 128 MiB of HBM per device.

```python
import math
import jax
import jax.numpy as jnp
from jax import lax

HEADS = 40
HD = 128
FT = 96
WF = 12
SF = 4
WINDOWS = 32
CTX = 16
ROWS = 1152
STRIDE = 8


def draw_query_tokens(key, part):
    key = jax.random.fold_in(key, 5)
    noise = jnp.clip(jax.random.normal(key, (WINDOWS, WF * FT, HEADS * HD), jnp.float32), -4.0, 4.0)
    result = noise
    return result.astype(jnp.bfloat16)


def draw_key_tokens(key, part):
    key = jax.random.fold_in(key, 7)
    noise = jnp.clip(jax.random.normal(key, (WINDOWS, WF * FT, HEADS * HD), jnp.float32), -4.0, 4.0)
    result = noise
    return result.astype(jnp.bfloat16)


def draw_context_index(key, part):
    key = jax.random.fold_in(key, 17)
    keys_all = jax.random.split(key, 7)
    window_ids_flat = jnp.arange(WINDOWS, dtype=jnp.int32)
    is_last = window_ids_flat == WINDOWS - 1
    first_kf = jax.random.randint(keys_all[0], (WINDOWS,), 0, WF)
    second_kf = (first_kf + jax.random.randint(keys_all[1], (WINDOWS,), 1, WF)) % WF
    first_kf = jnp.where(is_last, jnp.where(first_kf == WF - 1, 0, first_kf), first_kf)
    second_kf = jnp.where(is_last, WF - 1, second_kf)
    others = WINDOWS - 3
    rank_keys = jax.random.randint(keys_all[2], (WINDOWS, others), 0, 1 << 20) * others + jnp.arange(others, dtype=jnp.int32)[None, :]
    order = jnp.argsort(rank_keys, axis=1, stable=True).astype(jnp.int32)
    fixed_steps = jnp.broadcast_to(jnp.array([1, 2], jnp.int32), (WINDOWS, 2))
    steps_all = jnp.concatenate([fixed_steps, order + 3], axis=1)[:, :CTX]
    window_ids = window_ids_flat[:, None]
    source = (window_ids + steps_all) % WINDOWS
    slot_ids = jnp.arange(CTX, dtype=jnp.int32)[None, :]
    sides = jax.random.randint(keys_all[3], (WINDOWS, CTX), 0, 2)
    sides = jnp.where(slot_ids == 0, 0, jnp.where(slot_ids == 1, 1, sides))
    frame_idx = jnp.where(sides == 0, first_kf[source], second_kf[source])
    used = jax.random.randint(keys_all[4], (WINDOWS,), CTX - 3 * CTX // 8, CTX + 1)
    fullest = jax.random.randint(keys_all[5], (), 0, WINDOWS)
    sparsest = (fullest + 1) % WINDOWS
    used = jnp.where(window_ids_flat == fullest, CTX, used)
    used = jnp.where(window_ids_flat == sparsest, 2, used)
    entries = jnp.where(slot_ids < used[:, None], source * WF + frame_idx, -1)
    mix_keys = jax.random.randint(keys_all[6], (WINDOWS, CTX), 0, 1 << 20) * CTX + slot_ids
    shuffle = jnp.argsort(mix_keys, axis=1, stable=True)
    return jnp.take_along_axis(entries, shuffle, axis=1).astype(jnp.int32)


def draw_window_start(key, part):
    key = jax.random.fold_in(key, 23)
    window_ids = jnp.arange(WINDOWS, dtype=jnp.int32)
    jitter = jax.random.randint(key, (WINDOWS,), 0, STRIDE)
    jitter = jnp.where(window_ids == 0, 0, jnp.where(window_ids == WINDOWS - 1, STRIDE - 1, jitter))
    return (window_ids * STRIDE + jitter).astype(jnp.int32)


def block_scale(key, dims, shards, smallest, largest):
    gain = 1.0
    for axis_at, shards_of in shards:
        heights = jax.random.uniform(jax.random.fold_in(jax.random.fold_in(key, 6), axis_at), (shards_of,), jnp.float32, smallest / len(shards), largest / len(shards))
        gain = gain * jnp.repeat(jnp.exp(heights), dims[axis_at] // shards_of).reshape((-1,) + (1,) * (len(dims) - 1 - axis_at))
    return gain


def normal_values(key, extent, deviation, limit, cuts=(), kind=jnp.bfloat16):
    values = deviation * jax.random.normal(key, extent, jnp.float32)
    if cuts:
        values = values * block_scale(key, extent, cuts, -0.22, 0.18)
    return jnp.clip(values, -limit, limit).astype(kind)


def setup_inputs(seed: int = 0) -> dict:
    key_list = jax.random.split(jax.random.key(seed), 6)
    query_tokens = draw_query_tokens(jax.random.fold_in(key_list[5], 71), 0)
    key_tokens = draw_key_tokens(jax.random.fold_in(key_list[5], 71), 0)
    value_tokens = normal_values(key_list[2], (WINDOWS, ROWS, HEADS * HD), 1.0, 6.0, ((0, 32), (2, 8)))
    context_index = draw_context_index(jax.random.fold_in(key_list[5], 71), 0)
    window_start = draw_window_start(jax.random.fold_in(key_list[5], 71), 0)
    return dict(query_tokens=query_tokens, key_tokens=key_tokens, value_tokens=value_tokens, context_index=context_index, window_start=window_start)


def softmax_mix(scores, values):
    top_score = lax.optimization_barrier(jnp.max(scores, axis=-1, keepdims=True))
    exponent = jnp.exp(scores - top_score)
    totals = lax.optimization_barrier(jnp.sum(exponent, axis=-1, keepdims=True))
    rounded = lax.optimization_barrier(exponent.astype(jnp.bfloat16)).astype(jnp.float32)
    summed = jnp.einsum('hqk,khd->qhd', rounded, values.astype(jnp.float32))
    return summed / jnp.transpose(totals, (1, 0, 2))

def reference(query_tokens, key_tokens, value_tokens, context_index, window_start):
    row_count = WF * FT
    shared = SF * FT
    score_scale = 1.0 / math.sqrt(HD)
    slopes = 0.25 * jnp.exp2(-8.0 * jnp.arange(HEADS, dtype=jnp.float32) / HEADS)
    key_frames = key_tokens.reshape(WINDOWS * WF, FT, HEADS, HD)
    value_frames = value_tokens.reshape(WINDOWS * WF, FT, HEADS, HD)
    frame_of_row = jnp.arange(row_count, dtype=jnp.int32) // FT
    step_in = (jnp.arange(shared, dtype=jnp.int32) // FT).astype(jnp.float32)

    def one_window(window):
        queries = query_tokens[window].reshape(row_count, HEADS, HD).astype(jnp.float32)
        keys_own = key_tokens[window].reshape(row_count, HEADS, HD).astype(jnp.float32)
        values_own = value_tokens[window].reshape(row_count, HEADS, HD).astype(jnp.float32)
        entries = context_index[window]
        is_live = entries >= 0
        safe_idx = jnp.maximum(entries, 0).astype(jnp.int32)
        source = safe_idx // WF
        frame_idx = safe_idx % WF
        ctx_keys = key_frames[safe_idx].reshape(CTX * FT, HEADS, HD).astype(jnp.float32)
        ctx_values = value_frames[safe_idx].reshape(CTX * FT, HEADS, HD).astype(jnp.float32)
        query_pos = window_start[window] + frame_of_row
        key_pos = window_start[source] + frame_idx
        distance = jnp.abs(query_pos[:, None] - key_pos[None, :]).astype(jnp.float32)
        distance = jnp.repeat(distance, FT, axis=1)
        key_live = jnp.repeat(is_live, FT)
        ctx_bias = jnp.where(key_live[None, None, :], -slopes[:, None, None] * distance[None], -jnp.inf)
        own_scores = jnp.einsum('qhd,khd->hqk', queries, keys_own) * score_scale
        ctx_scores = jnp.einsum('qhd,khd->hqk', queries, ctx_keys) * score_scale + ctx_bias
        blended = softmax_mix(jnp.concatenate([own_scores, ctx_scores], axis=2), jnp.concatenate([values_own, ctx_values], axis=0))
        earlier_win = jnp.maximum(window - 1, 0)
        later_win = jnp.minimum(window + 1, WINDOWS - 1)
        left_keys = key_tokens[earlier_win, row_count - shared:].reshape(shared, HEADS, HD).astype(jnp.float32)
        left_values = value_tokens[earlier_win, row_count - shared:].reshape(shared, HEADS, HD).astype(jnp.float32)
        right_keys = key_tokens[later_win, :shared].reshape(shared, HEADS, HD).astype(jnp.float32)
        right_values = value_tokens[later_win, :shared].reshape(shared, HEADS, HD).astype(jnp.float32)
        cross_head = softmax_mix(jnp.einsum('qhd,khd->hqk', queries[:shared], left_keys) * score_scale, left_values)
        cross_tail = softmax_mix(jnp.einsum('qhd,khd->hqk', queries[row_count - shared:], right_keys) * score_scale, right_values)
        beta_head = jnp.where(window > 0, (step_in + 1.0) / (SF + 1.0), 1.0)[:, None, None]
        beta_tail = jnp.where(window < WINDOWS - 1, (SF - step_in) / (SF + 1.0), 1.0)[:, None, None]
        head_rows = beta_head * blended[:shared] + (1.0 - beta_head) * cross_head
        tail_rows = beta_tail * blended[row_count - shared:] + (1.0 - beta_tail) * cross_tail
        joined = jnp.concatenate([head_rows, blended[shared:row_count - shared], tail_rows], axis=0)
        return joined.reshape(row_count, HEADS * HD).astype(jnp.bfloat16)
    return lax.map(one_window, jnp.arange(WINDOWS, dtype=jnp.int32))
```

```python
import functools
import math

import jax
import jax.numpy as jnp
from jax import lax
from jax.experimental import pallas as pl
from jax.experimental.pallas import tpu as pltpu
from jax.sharding import PartitionSpec as P

HEADS = 40
HD = 128
FT = 96
WF = 12
SF = 4
ROWS = WF * FT
SH = SF * FT
CTX = 16
GROUP = 4
HERE = 5
WIDTH = HERE * HD
SCALE = math.log2(math.e) / math.sqrt(HD)
BF = jnp.bfloat16
F32 = jnp.float32
NT = (((1,), (1,)), ((), ()))
ROOM = pltpu.CompilerParams(vmem_limit_bytes=56 * 2**20)


def with_ones(values):
    return jnp.concatenate([values, jnp.ones((values.shape[0], HD), BF)], axis=1)


def mix(scores, values_ones):
    top = jnp.max(scores, axis=-1, keepdims=True)
    weights = jnp.exp2(scores - top).astype(BF)
    return jnp.dot(weights, values_ones, preferred_element_type=F32), top


def scored(queries, keys):
    return lax.dot_general(queries, keys, NT, preferred_element_type=F32) * SCALE


def share(side, frame):
    return (frame + 1.0) / (SF + 1.0) if side == 0 else (SF - frame) / (SF + 1.0)


def own_kernel(q_ref, k_ref, v_ref, out_ref, lse_ref, *, tile):
    values_ones = with_ones(v_ref[...])
    for i in range(ROWS // tile):
        rows = slice(i * tile, (i + 1) * tile)
        mixed, top = mix(scored(q_ref[rows], k_ref[...]), values_ones)
        total = mixed[:, HD:]
        out_ref[rows] = mixed[:, :HD] / total
        lse_ref[rows] = top + jnp.log2(total)


def own_attention(queries, keys, values):
    block = pl.BlockSpec((ROWS, HD), lambda h: (0, h))
    return pl.pallas_call(
        functools.partial(own_kernel, tile=384),
        grid=(HERE,),
        in_specs=[block] * 3,
        out_specs=[block] * 2,
        out_shape=[jax.ShapeDtypeStruct((ROWS, WIDTH), F32)] * 2,
        cost_estimate=pl.CostEstimate(
            flops=HERE * ROWS * ROWS * HD * 4,
            bytes_accessed=10 * 2**20,
            transcendentals=HERE * ROWS * ROWS,
        ),
        compiler_params=ROOM,
        name="own",
    )(queries, keys, values)


def cross_kernel(edge, q_ref, left_ref, right_ref, out_ref, *, tile):
    for side in range(2):
        both = (left_ref, right_ref)[side]
        values_ones = with_ones(both[SH:])
        live = (edge[side] > 0).astype(F32)
        for i in range(SH // tile):
            start = side * (ROWS - SH) + i * tile
            mixed, _ = mix(scored(q_ref[start : start + tile], both[:SH]), values_ones)
            crossed = mixed[:, :HD] / mixed[:, HD:]
            for f in range(tile // FT):
                j = i * (tile // FT) + f
                out_ref[side * SH + j * FT : side * SH + (j + 1) * FT] = crossed[
                    f * FT : (f + 1) * FT
                ] * (live * (1.0 - share(side, j)))


def cross_attention(edge, queries, left, right):
    q_block = pl.BlockSpec((ROWS, HD), lambda h, e: (0, h))
    block = pl.BlockSpec((2 * SH, HD), lambda h, e: (0, h))
    return pl.pallas_call(
        functools.partial(cross_kernel, tile=384),
        grid_spec=pltpu.PrefetchScalarGridSpec(
            num_scalar_prefetch=1,
            grid=(HERE,),
            in_specs=[q_block, block, block],
            out_specs=block,
        ),
        out_shape=jax.ShapeDtypeStruct((2 * SH, WIDTH), F32),
        cost_estimate=pl.CostEstimate(
            flops=HERE * 2 * SH * SH * HD * 4,
            bytes_accessed=7 * 2**20,
            transcendentals=HERE * 2 * SH * SH,
        ),
        compiler_params=ROOM,
        name="cross",
    )(edge, queries, left, right)


def context_kernel(
    place, edge, slope_ref, far_ref, q_ref, own_ref, lse_ref, cross_ref, frames_ref, out_ref,
    keys, values, sem, *, tile
):
    head = pl.program_id(0)
    used = edge[2]

    def copies(slot, h):
        lanes = pl.ds(pl.multiple_of(h * HD, HD), HD)
        rows = pl.ds(slot * FT, FT)
        window, which = place[slot], place[slot + CTX]
        return (
            pltpu.make_async_copy(
                frames_ref.at[window, which, :, lanes], keys.at[h, rows], sem.at[h]
            ),
            pltpu.make_async_copy(
                frames_ref.at[window, which + 2, :, lanes], values.at[h, rows], sem.at[h]
            ),
        )

    @pl.when(head == 0)
    def _():
        for h in range(HERE):
            for slot in range(CTX):

                @pl.when(slot < used)
                def _():
                    for copy in copies(slot, h):
                        copy.start()

                @pl.when(slot >= used)
                def _():
                    keys[h, slot * FT : (slot + 1) * FT] = jnp.zeros((FT, HD), BF)
                    values[h, slot * FT : (slot + 1) * FT] = jnp.zeros((FT, HD), BF)

    for slot in range(CTX):

        @pl.when(slot < used)
        def _():
            for copy in copies(slot, head):
                copy.wait()

    slope = slope_ref[head]
    per_tile = tile // FT

    def work(groups):
        width = groups * GROUP * FT
        k = keys[head, :width]
        values_ones = with_ones(values[head, :width])
        for i in range(ROWS // tile):
            rows = slice(i * tile, (i + 1) * tile)
            scores = scored(q_ref[rows], k)
            parts = [
                scores[f * FT : (f + 1) * FT]
                + far_ref[i * per_tile + f : i * per_tile + f + 1, :width] * slope
                for f in range(per_tile)
            ]
            mixed, top = mix(jnp.concatenate(parts, axis=0), values_ones)
            lse = lse_ref[rows]
            higher = jnp.maximum(lse, top)
            of_own = jnp.exp2(lse - higher)
            of_context = jnp.exp2(top - higher)
            out = (own_ref[rows] * of_own + mixed[:, :HD] * of_context) / (
                of_own + mixed[:, HD:] * of_context
            )
            for f in range(per_tile):
                j = i * per_tile + f
                piece = out[f * FT : (f + 1) * FT]
                side = 0 if j < SF else 1
                if j < SF or j >= WF - SF:
                    j_in = j if j < SF else j - (WF - SF)
                    live = (edge[side] > 0).astype(F32)
                    at = side * SH + j_in * FT
                    piece = piece * (1.0 - live * (1.0 - share(side, j_in)))
                    piece = piece + cross_ref[at : at + FT]
                out_ref[j * FT : (j + 1) * FT] = piece.astype(BF)

    for groups in range(1, CTX // GROUP + 1):

        @pl.when((used + GROUP - 1) // GROUP == groups)
        def _():
            work(groups)


def context_attention(place, edge, slopes, far, queries, own, lse, crossed, frames):
    block = pl.BlockSpec((ROWS, HD), lambda h, *_: (0, h))
    return pl.pallas_call(
        functools.partial(context_kernel, tile=192),
        grid_spec=pltpu.PrefetchScalarGridSpec(
            num_scalar_prefetch=3,
            grid=(HERE,),
            in_specs=[
                pl.BlockSpec((WF, CTX * FT), lambda h, *_: (0, 0)),
                block,
                block,
                block,
                pl.BlockSpec((2 * SH, HD), lambda h, *_: (0, h)),
                pl.BlockSpec(memory_space=pl.ANY),
            ],
            out_specs=block,
            scratch_shapes=[
                pltpu.VMEM((HERE, CTX * FT, HD), BF),
                pltpu.VMEM((HERE, CTX * FT, HD), BF),
                pltpu.SemaphoreType.DMA((HERE,)),
            ],
        ),
        out_shape=jax.ShapeDtypeStruct((ROWS, WIDTH), BF),
        cost_estimate=pl.CostEstimate(
            flops=HERE * ROWS * CTX * FT * HD * 4,
            bytes_accessed=14 * 2**20,
            transcendentals=HERE * ROWS * CTX * FT,
        ),
        compiler_params=ROOM,
        name="context",
    )(place, edge, slopes, far, queries, own, lse, crossed, frames)


def shifted(value, by):
    peers = lax.axis_size("win")
    pairs = [(i, i + by) for i in range(peers) if 0 <= i + by < peers]
    return lax.ppermute(value, "win", pairs)


def named_frames(context_index, win_id):
    asked = (context_index >= 0) & (context_index // WF == win_id)
    frame = context_index % WF
    low = jnp.min(jnp.where(asked, frame, WF))
    high = jnp.max(jnp.where(asked, frame, -1))
    return jnp.clip(low, 0, WF - 1), jnp.clip(high, 0, WF - 1)


def my_slots(context_index, window_start, win_id):
    windows = context_index.shape[0]
    entries = lax.dynamic_index_in_dim(context_index, win_id, 0, keepdims=False)
    live = entries >= 0
    at = jnp.cumsum(live.astype(jnp.int32)) - 1
    move = live[None, :] & (at[None, :] == jnp.arange(CTX, dtype=jnp.int32)[:, None])
    entries = jnp.sum(jnp.where(move, entries[None, :], 0), axis=1)
    used = jnp.sum(live.astype(jnp.int32))
    live = jnp.arange(CTX, dtype=jnp.int32) < used
    source = entries // WF
    frame = entries % WF
    names = (context_index >= 0)[None] & (context_index[None] // WF == source[:, None, None])
    low = jnp.min(jnp.where(names, context_index[None] % WF, WF), axis=(1, 2))
    which = (frame != low).astype(jnp.int32)
    from_table = source[:, None] == jnp.arange(windows, dtype=jnp.int32)[None, :]
    key_pos = jnp.sum(jnp.where(from_table, window_start[None, :], 0), axis=1) + frame
    my_start = lax.dynamic_index_in_dim(window_start, win_id, 0, keepdims=False)
    query_pos = my_start + jnp.arange(WF, dtype=jnp.int32)
    distance = jnp.abs(query_pos[:, None] - key_pos[None, :]).astype(F32)
    far = jnp.where(live[None, :], -distance, -1e30)
    far = jnp.broadcast_to(far[:, :, None], (WF, CTX, FT)).reshape(WF, CTX * FT)
    return jnp.concatenate([source, which]), used, far


def on_device(query_tokens, key_tokens, value_tokens, context_index, window_start):
    queries, keys, values = query_tokens[0], key_tokens[0], value_tokens[0]
    windows = lax.axis_size("win")
    win_id = lax.axis_index("win")
    low, high = named_frames(context_index, win_id)
    packed = jnp.concatenate(
        [
            lax.dynamic_slice_in_dim(array, frame * FT, FT, 0)
            for array in (keys, values)
            for frame in (low, high)
        ],
        axis=0,
    )
    frames = lax.all_gather(packed, "win", axis=0, tiled=True)
    frames = frames.reshape(windows, 4, FT, WIDTH)
    left = shifted(jnp.concatenate([keys[ROWS - SH :], values[ROWS - SH :]], axis=0), 1)
    right = shifted(jnp.concatenate([keys[:SH], values[:SH]], axis=0), -1)
    place, used, far = my_slots(context_index, window_start, win_id)
    edge = jnp.stack([win_id, windows - 1 - win_id, used]).astype(jnp.int32)
    head_ids = lax.axis_index("head") * HERE + jnp.arange(HERE, dtype=jnp.int32)
    slopes = 0.25 * math.log2(math.e) * jnp.exp2(-8.0 * head_ids.astype(F32) / HEADS)
    own, lse = own_attention(queries, keys, values)
    crossed = cross_attention(edge, queries, left, right)
    return context_attention(place, edge, slopes, far, queries, own, lse, crossed, frames)[None]


def solution(mesh):
    spec = P("win", None, "head")
    return jax.shard_map(
        on_device, mesh=mesh, in_specs=(spec, spec, spec, P(), P()), out_specs=spec, check_vma=False
    )
```

```python
import functools
import math

import jax
import jax.numpy as jnp
from jax import lax
from jax.experimental import pallas as pl
from jax.experimental.pallas import tpu as pltpu
from jax.sharding import PartitionSpec as P

HEADS = 40
HD = 128
FT = 96
WF = 12
SF = 4
ROWS = WF * FT
SH = SF * FT
CTX = 16
WINDOWS = 32
PLANES = 8
LANES = 128
LOW, START, WIN, HEAD = CTX, 2 * CTX, 2 * CTX + WINDOWS, 2 * CTX + WINDOWS + 1
HERE = 5
WIDTH = HERE * HD
SCALE = math.log2(math.e) / math.sqrt(HD)
BF = jnp.bfloat16
F32 = jnp.float32
NT = (((1,), (1,)), ((), ()))
ROOM = pltpu.CompilerParams(vmem_limit_bytes=56 * 2**20)


def placed(win):
    return win >> 2, win >> 1 & 1, win & 1


def lasting(microseconds):
    return pl.CostEstimate(flops=int(microseconds * 2e7), bytes_accessed=0, transcendentals=0)


def with_ones(values):
    return jnp.concatenate([values, jnp.ones((values.shape[0], HD), BF)], axis=1)


def mix(scores, values_ones):
    top = jnp.max(scores, axis=-1, keepdims=True)
    weights = jnp.exp2(scores - top).astype(BF)
    return jnp.dot(weights, values_ones, preferred_element_type=F32), top


def scored(queries, keys):
    return lax.dot_general(queries, keys, NT, preferred_element_type=F32) * SCALE


def share(side, frame):
    return (frame + 1.0) / (SF + 1.0) if side == 0 else (SF - frame) / (SF + 1.0)


def own_kernel(q_ref, k_ref, v_ref, out_ref, lse_ref, *, tile):
    values_ones = with_ones(v_ref[...])
    for i in range(ROWS // tile):
        rows = slice(i * tile, (i + 1) * tile)
        mixed, top = mix(scored(q_ref[rows], k_ref[...]), values_ones)
        total = mixed[:, HD:]
        out_ref[rows] = mixed[:, :HD] / total
        lse_ref[rows] = top + jnp.log2(total)


def own_attention(queries, keys, values, first, count, before=None):
    block = pl.BlockSpec((ROWS, HD), lambda h: (0, first + h))
    untouched = [] if before is None else [pl.BlockSpec(memory_space=pl.ANY)] * 2

    def kernel(q_ref, k_ref, v_ref, *refs):
        own_kernel(q_ref, k_ref, v_ref, refs[-2], refs[-1], tile=384)

    return pl.pallas_call(
        kernel,
        grid=(count,),
        in_specs=[block] * 3 + untouched,
        out_specs=[block] * 2,
        out_shape=[jax.ShapeDtypeStruct((ROWS, WIDTH), F32)] * 2,
        input_output_aliases={} if before is None else {3: 0, 4: 1},
        cost_estimate=lasting(1.0 + 3.0 * count),
        compiler_params=ROOM,
        name="own",
    )(queries, keys, values, *(() if before is None else before))


def has_side(info, side):
    return (info[WIN] != (0, WINDOWS - 1)[side]).astype(F32)


def cross_kernel(info, q_ref, left_ref, right_ref, out_ref, *, tile):
    for side in range(2):
        both = (left_ref, right_ref)[side]
        values_ones = with_ones(both[SH:])
        live = has_side(info, side)
        for i in range(SH // tile):
            start = side * (ROWS - SH) + i * tile
            mixed, _ = mix(scored(q_ref[start : start + tile], both[:SH]), values_ones)
            crossed = mixed[:, :HD] / mixed[:, HD:]
            for f in range(tile // FT):
                j = i * (tile // FT) + f
                out_ref[side * SH + j * FT : side * SH + (j + 1) * FT] = crossed[
                    f * FT : (f + 1) * FT
                ] * (live * (1.0 - share(side, j)))


def cross_attention(info, queries, left, right):
    q_block = pl.BlockSpec((ROWS, HD), lambda h, e: (0, h))
    block = pl.BlockSpec((2 * SH, HD), lambda h, e: (0, h))
    return pl.pallas_call(
        functools.partial(cross_kernel, tile=384),
        grid_spec=pltpu.PrefetchScalarGridSpec(
            num_scalar_prefetch=1,
            grid=(HERE,),
            in_specs=[q_block, block, block],
            out_specs=block,
        ),
        out_shape=jax.ShapeDtypeStruct((2 * SH, WIDTH), F32),
        cost_estimate=lasting(7.5),
        compiler_params=ROOM,
        name="cross",
    )(info, queries, left, right)


def plan(info, lists, most, wanted):
    z, x, core = placed(info[WIN])
    count = jnp.int32(0)
    for slot in range(CTX):
        entry = info[slot]
        source = jnp.maximum(entry, 0) // WF
        frame = entry - source * WF
        which = (frame != info[LOW + slot]).astype(jnp.int32)
        s_z, s_x, s_core = placed(source)
        other = (s_x != x).astype(jnp.int32)
        far_core = (s_core != core).astype(jnp.int32)
        away = (s_z - z) & (PLANES - 1)
        up = (away > 4).astype(jnp.int32)
        steps = jnp.where(up == 1, PLANES - away, away)
        swapped = jnp.where(up == 1, core, 1 - core)
        half = jnp.where(up == 1, s_core, 1 - s_core)
        array, start = wanted(source, steps, other, far_core, swapped, half)
        lists[count] = array
        lists[most + 1 + count] = start + which
        lists[2 * most + 2 + count] = info[START + source] + frame
        count = count + ((entry >= 0) & (array >= 0)).astype(jnp.int32)
    lists[3 * most + 3] = count


def everywhere(source, steps, other, far_core, swapped, half):
    at_home = jnp.where(other == 1, 1 + far_core, 0)
    array = jnp.where(steps == 4, 15 + other * 2 + far_core, 4 * steps - 1 + other * 2 + swapped)
    start = jnp.where((steps == 0) | (steps == 4), 0, half * 4)
    return jnp.where(steps == 0, at_home, array), start


def widths_of(most):
    return [w for w in range(2 * LANES, most * FT, 2 * LANES)] + [most * FT]


def context_kernel(info, q_ref, own_ref, lse_ref, *refs, tile, most, sources, wanted, last):
    cross_ref = refs[0] if last else None
    refs = refs[1:] if last else refs
    source_refs, refs = refs[:sources], refs[sources:]
    out_ref, lse_out_ref = (refs[0], None) if last else refs[:2]
    keys, values, far_ref, lists, sem = refs[-5:]
    head = pl.program_id(0)

    def copies(source, start, slot):
        rows = pl.ds(slot * FT, FT)
        k_rows = pl.ds(pl.multiple_of(start * FT, FT), FT)
        v_rows = pl.ds(pl.multiple_of((start + 2) * FT, FT), FT)
        return (
            pltpu.make_async_copy(source.at[k_rows], keys.at[rows], sem.at[0]),
            pltpu.make_async_copy(source.at[v_rows], values.at[rows], sem.at[1]),
        )

    @pl.when(head == 0)
    def _():
        plan(info, lists, most, wanted)
        used = lists[3 * most + 3]
        for slot in range(most):
            for s in range(sources):

                @pl.when((slot < used) & (lists[slot] == s))
                def _():
                    for copy in copies(source_refs[s], lists[most + 1 + slot], slot):
                        copy.start()

            @pl.when(slot >= used)
            def _():
                keys[slot * FT : (slot + 1) * FT] = jnp.zeros((FT, WIDTH), BF)
                values[slot * FT : (slot + 1) * FT] = jnp.zeros((FT, WIDTH), BF)

        lane = lax.broadcasted_iota(jnp.int32, (1, most * FT), 1)
        key_pos = jnp.zeros((1, most * FT), F32)
        for slot in range(most):
            here = jnp.where(slot < used, lists[2 * most + 2 + slot].astype(F32), 1e30)
            key_pos = jnp.where(lane >= slot * FT, here, key_pos)
        frame = lax.broadcasted_iota(jnp.int32, (WF, 1), 0)
        query_pos = (info[START + info[WIN]] + frame).astype(F32)
        far_ref[...] = -jnp.abs(query_pos - key_pos)

        for slot in range(most):

            @pl.when(slot < used)
            def _():
                for copy in copies(source_refs[0], 0, slot):
                    copy.wait()

    used = lists[3 * most + 3]
    lanes = pl.ds(pl.multiple_of(head * HD, HD), HD)
    which_head = (info[HEAD] + head).astype(F32)
    slope = jnp.exp2(jnp.full((1, LANES), -8.0 / HEADS, F32) * which_head)[:, :1]
    slope = slope * (0.25 * math.log2(math.e))
    per_tile = tile // FT

    def finish(i, out):
        for f in range(per_tile):
            j = i * per_tile + f
            piece = out[f * FT : (f + 1) * FT]
            side = 0 if j < SF else 1
            if j < SF or j >= WF - SF:
                j_in = j if j < SF else j - (WF - SF)
                at = side * SH + j_in * FT
                piece = piece * (1.0 - has_side(info, side) * (1.0 - share(side, j_in)))
                piece = piece + cross_ref[at : at + FT]
            out_ref[j * FT : (j + 1) * FT] = piece.astype(BF)

    def work(width):
        if width:
            k = keys[:width, lanes]
            values_ones = with_ones(values[:width, lanes])
        for i in range(ROWS // tile):
            rows = slice(i * tile, (i + 1) * tile)
            if not width:
                if last:
                    finish(i, own_ref[rows])
                else:
                    out_ref[rows] = own_ref[rows]
                    lse_out_ref[rows] = lse_ref[rows]
                continue
            scores = scored(q_ref[rows], k)
            parts = [
                scores[f * FT : (f + 1) * FT]
                + far_ref[i * per_tile + f : i * per_tile + f + 1, :width] * slope
                for f in range(per_tile)
            ]
            mixed, top = mix(jnp.concatenate(parts, axis=0), values_ones)
            lse = lse_ref[rows]
            higher = jnp.maximum(lse, top)
            of_own = jnp.exp2(lse - higher)
            of_context = jnp.exp2(top - higher)
            total = of_own + mixed[:, HD:] * of_context
            out = (own_ref[rows] * of_own + mixed[:, :HD] * of_context) / total
            if last:
                finish(i, out)
            else:
                out_ref[rows] = out
                lse_out_ref[rows] = higher + jnp.log2(total)

    below = 0
    for width in [0] + widths_of(most):
        fits = width // FT

        @pl.when((used <= fits) & (used >= below))
        def _():
            work(width)

        below = fits + 1


def context_attention(info, queries, state, sources, most, wanted, crossed=None):
    last = crossed is not None
    block = pl.BlockSpec((ROWS, HD), lambda h, *_: (0, h))
    cross_block = pl.BlockSpec((2 * SH, HD), lambda h, *_: (0, h))
    f32 = jax.ShapeDtypeStruct((ROWS, WIDTH), F32)
    return pl.pallas_call(
        functools.partial(
            context_kernel,
            tile=192,
            most=most,
            sources=len(sources),
            wanted=wanted,
            last=last,
        ),
        grid_spec=pltpu.PrefetchScalarGridSpec(
            num_scalar_prefetch=1,
            grid=(HERE,),
            in_specs=[block, block, block]
            + [cross_block] * last
            + [pl.BlockSpec(memory_space=pl.ANY)] * len(sources),
            out_specs=block if last else [block, block],
            scratch_shapes=[
                pltpu.VMEM((most * FT, WIDTH), BF),
                pltpu.VMEM((most * FT, WIDTH), BF),
                pltpu.VMEM((WF, most * FT), F32),
                pltpu.SMEM((3 * most + 4,), jnp.int32),
                pltpu.SemaphoreType.DMA((2,)),
            ],
        ),
        out_shape=jax.ShapeDtypeStruct((ROWS, WIDTH), BF) if last else [f32, f32],
        cost_estimate=lasting(17.0),
        compiler_params=ROOM,
        name="context",
    )(info, queries, *state, *([crossed] * last), *sources)


def moved(value, move):
    peers = lax.axis_size("win")

    def target(win):
        z, x, core = move(*placed(win))
        return z % (peers // 4) * 4 + x * 2 + core

    return lax.ppermute(value, "win", [(i, target(i)) for i in range(peers)])


def round_z(value):
    return moved(value, lambda z, x, core: (z + 1 - 2 * core, x, core))


def to_sibling(value):
    return moved(value, lambda z, x, core: (z, x, 1 - core))


def to_partner(value):
    return moved(value, lambda z, x, core: (z, 1 - x, core))


def shifted(value, by):
    peers = lax.axis_size("win")
    pairs = [(i, i + by) for i in range(peers) if 0 <= i + by < peers]
    return lax.ppermute(value, "win", pairs)


def pack_kernel(index_ref, keys_ref, values_ref, out_ref, sem):
    first = lax.axis_index("win") * WF
    entries = index_ref[...]
    asked = (entries >= first) & (entries < first + WF)
    low = jnp.min(jnp.where(asked, entries - first, WF))
    high = jnp.max(jnp.where(asked, entries - first, -1))
    copies = []
    for source in (keys_ref, values_ref):
        for frame in (low, high):
            start = pl.multiple_of(jnp.clip(frame, 0, WF - 1) * FT, FT)
            at = len(copies)
            copies.append(
                pltpu.make_async_copy(
                    source.at[pl.ds(start, FT)], out_ref.at[pl.ds(at * FT, FT)], sem.at[at]
                )
            )
    for copy in copies:
        copy.start()
    for copy in copies:
        copy.wait()


def packed(context_index, keys, values):
    anywhere = pl.BlockSpec(memory_space=pl.ANY)
    return pl.pallas_call(
        pack_kernel,
        in_specs=[pl.BlockSpec(memory_space=pltpu.VMEM), anywhere, anywhere],
        out_specs=pl.BlockSpec(memory_space=pltpu.VMEM),
        out_shape=jax.ShapeDtypeStruct((4 * FT, WIDTH), BF),
        scratch_shapes=[pltpu.SemaphoreType.DMA((4,))],
        name="pack",
    )(context_index, keys, values)


def slot_info(context_index, window_start):
    win_id = lax.axis_index("win")
    entries = lax.dynamic_index_in_dim(context_index, win_id, 0, keepdims=False)
    first = jnp.maximum(entries, 0) // WF * WF
    frame = context_index[None] - first[:, None, None]
    low = jnp.min(jnp.where((frame >= 0) & (frame < WF), frame, WF), axis=(1, 2))
    ids = jnp.stack([win_id, lax.axis_index("head") * HERE]).astype(jnp.int32)
    return jnp.concatenate([entries, low, window_start, ids])


def together(*values):
    return lax.optimization_barrier(values)


def on_device(query_tokens, key_tokens, value_tokens, context_index, window_start):
    queries, keys, values = query_tokens[0], key_tokens[0], value_tokens[0]
    mine = packed(context_index, keys, values)
    sibling = to_sibling(mine)
    partner = to_partner(mine)
    info = slot_info(context_index, window_start)
    one0 = jnp.concatenate([mine, sibling], axis=0)
    one1 = round_z(one0)
    last_rows = jnp.concatenate([keys[ROWS - SH :], values[ROWS - SH :]], axis=0)
    first_rows = jnp.concatenate([keys[:SH], values[:SH]], axis=0)
    _, first_queries, last_rows, first_rows = together(one0, queries, last_rows, first_rows)
    left, right = shifted(last_rows, 1), shifted(first_rows, -1)
    state = own_attention(first_queries, keys, values, 0, 3)
    one1, partner, *state = together(one1, partner, *state)
    one2 = round_z(one1)
    partner_sibling = to_sibling(partner)
    two0 = jnp.concatenate([partner, partner_sibling], axis=0)
    two1 = round_z(two0)
    one1_back = to_sibling(one1)
    _, *state = together(two0, *state)
    state = own_attention(queries, keys, values, 3, 2, state)
    one2, *state = together(one2, *state)
    one3 = round_z(one2)
    one2_back = to_sibling(one2)
    two2 = round_z(two1)
    two1_back = to_sibling(two1)
    one4 = round_z(one3[: 4 * FT])
    one3_back = to_sibling(one3)
    _, left, right = together(two1, left, right)
    crossed = cross_attention(info, queries, left, right)
    two2, crossed = together(two2, crossed)
    two3 = round_z(two2)
    two2_back = to_sibling(two2)
    two4 = round_z(two3[: 4 * FT])
    two3_back = to_sibling(two3)
    one4_back = to_sibling(one4)
    two4_back = to_sibling(two4)
    out = context_attention(
        info,
        queries,
        state,
        [sibling, partner, partner_sibling]
        + [one1, one1_back, two1, two1_back, one2, one2_back, two2, two2_back]
        + [one3, one3_back, two3, two3_back, one4, one4_back, two4, two4_back],
        CTX,
        everywhere,
        crossed,
    )
    return out[None]


def solution(mesh):
    spec = P("win", None, "head")
    return jax.shard_map(
        on_device, mesh=mesh, in_specs=(spec, spec, spec, P(), P()), out_specs=spec, check_vma=False
    )
```
